32 devices in a mesh: span: 4 (over x, core), wall: 8 (over z, y).
Axes of the slice: x: 2, y: 2, z: 4, core: 2. Of those that a mesh axis runs over, the one named last changes fastest.
Arguments:
- velocity: float32 [3, 256, 128, 128], P(None, 'wall', 'span'), may hold values from -6 to 6
Outputs:
- velocity_next: float32 [3, 256, 128, 128], P(None, 'wall', 'span')
The draws below stay inside these ranges and needn't reach their ends.
All inputs are finite; a program needn't handle non-finite values.
Results may differ from the reference program's by a relative error of at most 0.0005.
Values sent between devices are 32-bit elements; how exact they have to be, the bound alone decides.
A program may use at most 64 MiB of HBM per device.

```python
import jax
import jax.numpy as jnp
from jax import lax

CX = 128
NY = 256
NZ = 128


def level_of(stream_key, dims, shards, least, high):
    def one(position, shards_of):
        steps = jax.random.uniform(jax.random.fold_in(jax.random.fold_in(stream_key, 6), position), (shards_of,), jnp.float32, least / len(shards), high / len(shards))
        return jnp.repeat(jnp.exp(steps), dims[position] // shards_of).reshape((-1,) + (1,) * (len(dims) - position - 1))

    gain = one(*shards[0])
    for cut in shards[1:]:
        gain = gain * one(*cut)
    return gain


def gaussian(stream_key, dims, scale, most, shards=(), dtype=jnp.bfloat16):
    array = jax.random.normal(stream_key, dims, jnp.float32) * scale
    if len(shards) > 0:
        array = level_of(stream_key, dims, shards, -0.22, 0.18) * array
    return jnp.clip(array, min=-most, max=most).astype(dtype)


def setup_inputs(seed: int = 0) -> dict:
    key_list = jax.random.split(jax.random.key(seed), 2)
    velocity = gaussian(key_list[0], (3, NY, NZ, CX), 1.0, 6.0, ((1, 8), (2, 4)), jnp.float32)
    return dict(velocity=velocity)


visc_base = 4000.0
smag_gain = 2000.0
adv_step = 0.2

def prepare(velocity, along_x, along_y, along_z):
    grads = (along_x, along_y, along_z)
    squares = jnp.zeros_like(velocity[0])
    for i in range(3):
        for j in range(3):
            strain = 0.5 * (grads[j][i] + grads[i][j])
            squares = squares + strain * strain
    strain_mag = jnp.sqrt(2.0 * squares)
    coupling = visc_base + smag_gain * strain_mag
    advect = velocity[0] * along_x + velocity[1] * along_y + velocity[2] * along_z
    return (velocity - adv_step * advect, coupling)

def reference(velocity):
    along_x = 0.5 * (jnp.roll(velocity, -1, axis=3) - jnp.roll(velocity, 1, axis=3))
    along_z = 0.5 * (jnp.roll(velocity, -1, axis=2) - jnp.roll(velocity, 1, axis=2))
    padded = jnp.pad(velocity, ((0, 0), (1, 1), (0, 0), (0, 0)))
    along_y = 0.5 * (padded[:, 2:] - padded[:, :-2])
    right_side, coupling = prepare(velocity, along_x, along_y, along_z)
    moved = jnp.moveaxis(right_side, 1, 0)
    links = coupling[:, None]

    def forward(carry, item):
        upper_prev, shifted_prev = carry
        source, k = item
        denom = 1.0 + 2.0 * k + k * upper_prev
        upper = -k / denom
        shifted = (source + k * shifted_prev) / denom
        return ((upper, shifted), (upper, shifted))
    start = jnp.zeros(moved.shape[1:], jnp.float32)
    _, (uppers, shifteds) = lax.scan(forward, (start, start), (moved, links))

    def backward(x_next, item):
        upper, shifted = item
        value = shifted - upper * x_next
        return (value, value)
    _, values = lax.scan(backward, start, (uppers, shifteds), reverse=True)
    return jnp.moveaxis(values, 0, 1)
```

```python
import functools

import jax
import jax.numpy as jnp
from jax import lax
from jax.experimental import pallas as pl
from jax.experimental.pallas import tpu as pltpu
from jax.sharding import PartitionSpec as P

visc_base = 4000.0
smag_gain = 2000.0
adv_step = 0.2

MESH = pl.DeviceIdType.MESH


def inverse(x):
    guess = pl.reciprocal(x, approx=True)
    return guess * (2.0 - x * guess)


def kernel(
    n, m, vel, out, ext, zsend, zlo, zhi, fac_u, fac_p, fac_s, part, parts, ends, sides, planes,
    load_sem, zs_sem, zr_sem, ys_sem, yr_sem, ps_sem, pr_sem, es_sem, er_sem, out_sem,
):
    _, ny, nz, nx = vel.shape
    rows = nz // n
    me = lax.axis_index("wall")
    mine = lax.axis_index("span")
    after, before = lax.rem(mine + 1, m), lax.rem(mine + m - 1, m)

    load = pltpu.make_async_copy(vel, ext.at[:, pl.ds(1, ny)], load_sem)
    load.start()

    barrier = pltpu.get_barrier_semaphore()
    for hop in range(1, n):
        pl.semaphore_signal(
            barrier, inc=1, device_id={"wall": lax.rem(me + hop, n)}, device_id_type=MESH
        )
    for peer in (after, before):
        pl.semaphore_signal(barrier, inc=1, device_id={"span": peer}, device_id_type=MESH)
    pl.semaphore_wait(barrier, n + 1)

    up = pltpu.make_async_remote_copy(
        vel.at[:, ny - 1], ext.at[:, 0], ys_sem.at[0], yr_sem.at[0],
        device_id={"wall": jnp.minimum(me + 1, n - 1)}, device_id_type=MESH,
    )
    down = pltpu.make_async_remote_copy(
        vel.at[:, 0], ext.at[:, ny + 1], ys_sem.at[1], yr_sem.at[1],
        device_id={"wall": jnp.maximum(me - 1, 0)}, device_id_type=MESH,
    )
    has_above = me < n - 1
    has_below = me > 0
    load.wait()

    for c in range(3):
        zsend[0, c] = ext[c, pl.ds(1, ny), 0, :]
        zsend[1, c] = ext[c, pl.ds(1, ny), nz - 1, :]
    to_after = pltpu.make_async_remote_copy(
        zsend.at[1], zlo, zs_sem.at[1], zr_sem.at[1],
        device_id={"span": after}, device_id_type=MESH,
    )
    to_before = pltpu.make_async_remote_copy(
        zsend.at[0], zhi, zs_sem.at[0], zr_sem.at[0],
        device_id={"span": before}, device_id_type=MESH,
    )
    to_after.start()
    to_before.start()
    pl.when(has_above)(up.start)
    pl.when(has_below)(down.start)

    depth = lax.broadcasted_iota(jnp.int32, (nz, nx), 0)
    is_first = depth == 0
    is_last = depth == nz - 1

    def prepare(y):
        v, hx, hy, hz = [], [], [], []
        for c in range(3):
            here = ext[c, y + 1]
            v.append(here)
            hx.append(pltpu.roll(here, nx - 1, 1) - pltpu.roll(here, 1, 1))
            hy.append(ext[c, y + 2] - ext[c, y])
            ahead = jnp.where(is_last, zhi[c, pl.ds(y, 1)], pltpu.roll(here, nz - 1, 0))
            behind = jnp.where(is_first, zlo[c, pl.ds(y, 1)], pltpu.roll(here, 1, 0))
            hz.append(ahead - behind)
        xy = hx[1] + hy[0]
        xz = hx[2] + hz[0]
        yz = hy[2] + hz[1]
        squares = 2.0 * (hx[0] * hx[0] + hy[1] * hy[1] + hz[2] * hz[2])
        squares = squares + (xy * xy + xz * xz + yz * yz)
        strain = squares * lax.rsqrt(jnp.maximum(squares, 1e-30))
        e = inverse(visc_base + (0.5 * smag_gain) * strain)
        f = []
        for c in range(3):
            advect = v[0] * hx[c] + v[1] * hy[c] + v[2] * hz[c]
            f.append((v[c] - (0.5 * adv_step) * advect) * e)
        return e, f

    def step(y, carry):
        w, p, left, s, a = carry
        e, f = prepare(y)
        t = e + w
        u = inverse(1.0 + t)
        w = t * u
        s = tuple((s[c] + f[c]) * u for c in range(3))
        a = tuple(a[c] + p * s[c] for c in range(3))
        p_new = p * u
        left = left - p * p_new
        fac_u[y] = u
        fac_p[y] = p_new
        for c in range(3):
            fac_s[c, y] = s[c]
        return w, p_new, left, s, a

    to_after.wait_recv()
    to_before.wait_recv()
    one = jnp.ones((nz, nx), jnp.float32)
    zero = jnp.zeros((nz, nx), jnp.float32)
    carry = (one, one, one, (zero,) * 3, (zero,) * 3)
    carry = lax.fori_loop(1, ny - 1, step, carry)

    @pl.when(has_above)
    def _():
        down.wait_recv()

    @pl.when(has_below)
    def _():
        up.wait_recv()

    @pl.when(jnp.logical_not(has_above))
    def _():
        ext[:, ny + 1] = jnp.zeros((3, nz, nx), jnp.float32)

    @pl.when(jnp.logical_not(has_below))
    def _():
        ext[:, 0] = jnp.zeros((3, nz, nx), jnp.float32)

    w, p, left, s, a = step(ny - 1, carry)
    e, f = prepare(0)
    values = (e + left, w, p, *s, *(f[c] + a[c] for c in range(3)))
    for k in range(n):
        for j, value in enumerate(values):
            part[k, j * rows : (j + 1) * rows] = value[k * rows : (k + 1) * rows]

    def spread(src, dst, send, recv):
        copies = []
        for hop in range(1, n):
            to = lax.rem(me + hop, n)
            copies.append(
                pltpu.make_async_remote_copy(
                    src.at[to], dst.at[me], send.at[to], recv.at[me],
                    device_id={"wall": to}, device_id_type=MESH,
                )
            )
        return copies

    def arrived(src, dst, send, recv, k):
        @pl.when(me != k)
        def _():
            pltpu.make_async_remote_copy(
                src.at[k], dst.at[k], send.at[k], recv.at[k],
                device_id={"wall": k}, device_id_type=MESH,
            ).wait_recv()

    first = spread(part, parts, ps_sem, pr_sem)
    for copy in first:
        copy.start()
    parts[me] = part[me]

    def item(k, j):
        return parts[k, j * rows : (j + 1) * rows]

    ratios, shifts = [], []
    for k in range(n):
        arrived(part, parts, ps_sem, pr_sem, k)
        if k == 0:
            scale = inverse(item(0, 0) + 1.0)
            shift = [item(0, 6 + c) * scale for c in range(3)]
        else:
            p_low = item(k - 1, 2)
            scale = inverse(item(k, 0) + (item(k - 1, 1) - p_low * ratios[-1]))
            shift = [
                (item(k, 6 + c) + item(k - 1, 3 + c) + p_low * shifts[-1][c]) * scale
                for c in range(3)
            ]
        ratios.append(item(k, 2) * scale)
        shifts.append(shift)
    above = [jnp.zeros((rows, nx), jnp.float32)] * 3
    for k in reversed(range(n)):
        here = [shifts[k][c] + ratios[k] * above[c] for c in range(3)]
        for c in range(3):
            ends[k, c * rows : (c + 1) * rows] = here[c]
            ends[k, (3 + c) * rows : (4 + c) * rows] = above[c]
        above = here
    second = spread(ends, sides, es_sem, er_sem)
    for copy in second:
        copy.start()
    sides[me] = ends[me]
    for k in range(n):
        arrived(ends, sides, es_sem, er_sem, k)
        for j in range(6):
            planes[j, k * rows : (k + 1) * rows] = sides[k, j * rows : (j + 1) * rows]

    base = tuple(planes[c] for c in range(3))

    def back(i, x):
        y = ny - 1 - i
        u = fac_u[y]
        p = fac_p[y]
        x = tuple(fac_s[c, y] + p * base[c] + u * x[c] for c in range(3))
        for c in range(3):
            fac_s[c, y] = x[c]
        return x

    lax.fori_loop(0, ny - 1, back, tuple(planes[3 + c] for c in range(3)))
    for c in range(3):
        fac_s[c, 0] = base[c]
    store = pltpu.make_async_copy(fac_s, out, out_sem)
    store.start()

    to_after.wait_send()
    to_before.wait_send()
    pl.when(has_above)(up.wait_send)
    pl.when(has_below)(down.wait_send)
    for copy in first + second:
        copy.wait_send()
    store.wait()


def body(n, m, velocity):
    _, ny, nz, nx = velocity.shape
    rows = nz // n
    f32 = jnp.float32
    dma = pltpu.SemaphoreType.DMA
    return pl.pallas_call(
        functools.partial(kernel, n, m),
        out_shape=jax.ShapeDtypeStruct(velocity.shape, f32),
        in_specs=[pl.BlockSpec(memory_space=pl.ANY)],
        out_specs=pl.BlockSpec(memory_space=pl.ANY),
        scratch_shapes=[
            pltpu.VMEM((3, ny + 2, nz, nx), f32),
            pltpu.VMEM((2, 3, ny, nx), f32),
            pltpu.VMEM((3, ny, nx), f32),
            pltpu.VMEM((3, ny, nx), f32),
            pltpu.VMEM((ny, nz, nx), f32),
            pltpu.VMEM((ny, nz, nx), f32),
            pltpu.VMEM((3, ny, nz, nx), f32),
            pltpu.VMEM((n, 9 * rows, nx), f32),
            pltpu.VMEM((n, 9 * rows, nx), f32),
            pltpu.VMEM((n, 6 * rows, nx), f32),
            pltpu.VMEM((n, 6 * rows, nx), f32),
            pltpu.VMEM((6, nz, nx), f32),
            dma,
            dma((2,)),
            dma((2,)),
            dma((2,)),
            dma((2,)),
            dma((n,)),
            dma((n,)),
            dma((n,)),
            dma((n,)),
            dma,
        ],
        compiler_params=pltpu.CompilerParams(
            collective_id=0, has_side_effects=True, vmem_limit_bytes=32 * 1024 * 1024
        ),
        name="channel",
    )(velocity)


def solution(mesh):
    n, m = mesh.shape["wall"], mesh.shape["span"]
    spec = P(None, "wall", "span", None)
    return jax.shard_map(
        functools.partial(body, n, m), mesh=mesh, in_specs=(spec,), out_specs=spec, check_vma=False
    )
```

```python
import functools

import jax
import jax.numpy as jnp
from jax import lax
from jax.experimental import pallas as pl
from jax.experimental.pallas import tpu as pltpu
from jax.sharding import PartitionSpec as P

visc_base = 4000.0
smag_gain = 2000.0
adv_step = 0.2

MESH = pl.DeviceIdType.MESH
TILE = 8


def inverse(x):
    guess = pl.reciprocal(x, approx=True)
    return guess * (2.0 - x * guess)


def kernel(
    n, m, vel, out, ext, zsend, zlo, zhi, fac_u, fac_p, fac_s, part, parts, ends, sides, planes,
    load_sem, zs_sem, zr_sem, ys_sem, yr_sem, ps_sem, pr_sem, es_sem, er_sem,
):
    _, ny, nz, nx = vel.shape
    rows = nz // n
    me = lax.axis_index("wall")
    mine = lax.axis_index("span")
    def peer(hop):
        if n & (n - 1):
            return lax.rem(me + hop, n)
        other = me
        for bit in (1 << i for i in range(n.bit_length() - 1)):
            if (n - hop) & bit:
                other = other + bit - 2 * bit * ((me // bit) % 2)
        return other

    after, before = lax.rem(mine + 1, m), lax.rem(mine + m - 1, m)

    load = pltpu.make_async_copy(vel, ext.at[:, pl.ds(1, ny), pl.ds(TILE, nz)], load_sem)
    load.start()

    barrier = pltpu.get_barrier_semaphore()
    for hop in range(1, n):
        pl.semaphore_signal(barrier, inc=1, device_id={"wall": peer(hop)}, device_id_type=MESH)
    for side in (after, before):
        pl.semaphore_signal(barrier, inc=1, device_id={"span": side}, device_id_type=MESH)

    load.wait()
    for c in range(3):
        zsend[0, c] = ext[c, pl.ds(1, ny), TILE, :]
        zsend[1, c] = ext[c, pl.ds(1, ny), TILE + nz - 1, :]
    pl.semaphore_wait(barrier, n + 1)
    to_after = pltpu.make_async_remote_copy(
        zsend.at[1], zlo, zs_sem.at[1], zr_sem.at[1],
        device_id={"span": after}, device_id_type=MESH,
    )
    to_before = pltpu.make_async_remote_copy(
        zsend.at[0], zhi, zs_sem.at[0], zr_sem.at[0],
        device_id={"span": before}, device_id_type=MESH,
    )
    to_after.start()
    to_before.start()

    up = pltpu.make_async_remote_copy(
        vel.at[:, ny - 1], ext.at[:, 0, pl.ds(TILE, nz)], ys_sem.at[0], yr_sem.at[0],
        device_id={"wall": jnp.minimum(me + 1, n - 1)}, device_id_type=MESH,
    )
    down = pltpu.make_async_remote_copy(
        vel.at[:, 0], ext.at[:, ny + 1, pl.ds(TILE, nz)], ys_sem.at[1], yr_sem.at[1],
        device_id={"wall": jnp.maximum(me - 1, 0)}, device_id_type=MESH,
    )
    has_above = me < n - 1
    has_below = me > 0
    pl.when(has_above)(up.start)
    pl.when(has_below)(down.start)

    def prepare(y, z):
        v, hx, hy, hz = [], [], [], []
        for c in range(3):
            here = ext[c, y + 1, z + TILE : z + 2 * TILE]
            v.append(here)
            hx.append(pltpu.roll(here, nx - 1, 1) - pltpu.roll(here, 1, 1))
            hy.append(
                ext[c, y + 2, z + TILE : z + 2 * TILE] - ext[c, y, z + TILE : z + 2 * TILE]
            )
            hz.append(
                ext[c, y + 1, z + TILE + 1 : z + 2 * TILE + 1]
                - ext[c, y + 1, z + TILE - 1 : z + 2 * TILE - 1]
            )
        xy = hx[1] + hy[0]
        xz = hx[2] + hz[0]
        yz = hy[2] + hz[1]
        squares = 2.0 * (hx[0] * hx[0] + hy[1] * hy[1] + hz[2] * hz[2])
        squares = squares + (xy * xy + xz * xz + yz * yz)
        strain = squares * lax.rsqrt(jnp.maximum(squares, 1e-30))
        e = inverse(visc_base + (0.5 * smag_gain) * strain)
        f = []
        for c in range(3):
            advect = v[0] * hx[c] + v[1] * hy[c] + v[2] * hz[c]
            f.append((v[c] - (0.5 * adv_step) * advect) * e)
        return e, f

    def step(y, z, carry):
        w, p, left, s, a = carry
        e, f = prepare(y, z)
        t = e + w
        u = inverse(1.0 + t)
        w = t * u
        s = tuple((s[c] + f[c]) * u for c in range(3))
        a = tuple(a[c] + p * s[c] for c in range(3))
        p_new = p * u
        left = left - p * p_new
        fac_u[y, z : z + TILE] = u
        fac_p[y, z : z + TILE] = p_new
        for c in range(3):
            fac_s[c, y, z : z + TILE] = s[c]
        return w, p_new, left, s, a

    one = jnp.ones((TILE, nx), jnp.float32)
    zero = jnp.zeros((TILE, nx), jnp.float32)
    start = (one, one, one, (zero,) * 3, (zero,) * 3)
    burst = 3 if (ny - 2) % 3 == 0 else 1

    def sweep(zs):
        def some(i, carries):
            for k in range(burst):
                carries = tuple(
                    step(1 + i * burst + k, z, carry) for z, carry in zip(zs, carries)
                )
            return carries

        return lax.fori_loop(0, (ny - 2) // burst, some, (start,) * len(zs))

    inner = tuple(range(TILE, nz - TILE, TILE))
    outer = (0, nz - TILE)
    carries = dict(zip(inner, sweep(inner)))

    to_after.wait_recv()
    to_before.wait_recv()
    for c in range(3):
        ext[c, pl.ds(1, ny), TILE - 1, :] = zlo[c]
        ext[c, pl.ds(1, ny), TILE + nz, :] = zhi[c]
    carries.update(zip(outer, sweep(outer)))

    @pl.when(has_above)
    def _():
        down.wait_recv()

    @pl.when(has_below)
    def _():
        up.wait_recv()

    @pl.when(jnp.logical_not(has_above))
    def _():
        ext[:, ny + 1, TILE : TILE + nz] = jnp.zeros((3, nz, nx), jnp.float32)

    @pl.when(jnp.logical_not(has_below))
    def _():
        ext[:, 0, TILE : TILE + nz] = jnp.zeros((3, nz, nx), jnp.float32)

    for z in range(0, nz, TILE):
        w, p, left, s, a = step(ny - 1, z, carries[z])
        e, f = prepare(0, z)
        values = (e + left, w, p, *s, *(f[c] + a[c] for c in range(3)))
        for k in range(z // rows, (z + TILE) // rows):
            for j, value in enumerate(values):
                part[k, j * rows : (j + 1) * rows] = value[k * rows - z : (k + 1) * rows - z]

    def spread(src, dst, send, recv):
        copies = []
        for hop in range(1, n):
            to = peer(hop)
            copies.append(
                pltpu.make_async_remote_copy(
                    src.at[to], dst.at[me], send.at[to], recv.at[me],
                    device_id={"wall": to}, device_id_type=MESH,
                )
            )
        return copies

    def arrived(src, dst, send, recv, k):
        @pl.when(me != k)
        def _():
            pltpu.make_async_remote_copy(
                src.at[k], dst.at[k], send.at[k], recv.at[k],
                device_id={"wall": k}, device_id_type=MESH,
            ).wait_recv()

    first = spread(part, parts, ps_sem, pr_sem)
    for copy in first:
        copy.start()
    parts[me] = part[me]

    def item(k, j):
        return parts[k, j * rows : (j + 1) * rows]

    ratios, shifts = [], []
    for k in range(n):
        arrived(part, parts, ps_sem, pr_sem, k)
        if k == 0:
            scale = inverse(item(0, 0) + 1.0)
            shift = [item(0, 6 + c) * scale for c in range(3)]
        else:
            p_low = item(k - 1, 2)
            scale = inverse(item(k, 0) + (item(k - 1, 1) - p_low * ratios[-1]))
            shift = [
                (item(k, 6 + c) + item(k - 1, 3 + c) + p_low * shifts[-1][c]) * scale
                for c in range(3)
            ]
        ratios.append(item(k, 2) * scale)
        shifts.append(shift)
    above = [jnp.zeros((rows, nx), jnp.float32)] * 3
    for k in reversed(range(n)):
        here = [shifts[k][c] + ratios[k] * above[c] for c in range(3)]
        for c in range(3):
            ends[k, c * rows : (c + 1) * rows] = here[c]
            ends[k, (3 + c) * rows : (4 + c) * rows] = above[c]
        above = here
    second = spread(ends, sides, es_sem, er_sem)
    for copy in second:
        copy.start()
    sides[me] = ends[me]
    for k in range(n):
        arrived(ends, sides, es_sem, er_sem, k)
        for j in range(6):
            planes[j, k * rows : (k + 1) * rows] = sides[k, j * rows : (j + 1) * rows]

    base = tuple(planes[c] for c in range(3))

    def back(i, x):
        y = ny - 1 - i
        u = fac_u[y]
        p = fac_p[y]
        x = tuple(fac_s[c, y] + p * base[c] + u * x[c] for c in range(3))
        for c in range(3):
            out[c, y] = x[c]
        return x

    lax.fori_loop(0, ny - 1, back, tuple(planes[3 + c] for c in range(3)))
    for c in range(3):
        out[c, 0] = base[c]

    to_after.wait_send()
    to_before.wait_send()
    pl.when(has_above)(up.wait_send)
    pl.when(has_below)(down.wait_send)
    for copy in first + second:
        copy.wait_send()


def body(n, m, velocity):
    _, ny, nz, nx = velocity.shape
    rows = nz // n
    f32 = jnp.float32
    dma = pltpu.SemaphoreType.DMA
    return pl.pallas_call(
        functools.partial(kernel, n, m),
        out_shape=jax.ShapeDtypeStruct(velocity.shape, f32),
        in_specs=[pl.BlockSpec(memory_space=pltpu.HBM)],
        out_specs=pl.BlockSpec(memory_space=pltpu.VMEM),
        scratch_shapes=[
            pltpu.VMEM((3, ny + 2, nz + 2 * TILE, nx), f32),
            pltpu.VMEM((2, 3, ny, nx), f32),
            pltpu.VMEM((3, ny, nx), f32),
            pltpu.VMEM((3, ny, nx), f32),
            pltpu.VMEM((ny, nz, nx), f32),
            pltpu.VMEM((ny, nz, nx), f32),
            pltpu.VMEM((3, ny, nz, nx), f32),
            pltpu.VMEM((n, 9 * rows, nx), f32),
            pltpu.VMEM((n, 9 * rows, nx), f32),
            pltpu.VMEM((n, 6 * rows, nx), f32),
            pltpu.VMEM((n, 6 * rows, nx), f32),
            pltpu.VMEM((6, nz, nx), f32),
            dma,
            dma((2,)),
            dma((2,)),
            dma((2,)),
            dma((2,)),
            dma((n,)),
            dma((n,)),
            dma((n,)),
            dma((n,)),
        ],
        compiler_params=pltpu.CompilerParams(
            collective_id=0, has_side_effects=True, vmem_limit_bytes=32 * 1024 * 1024
        ),
        name="channel",
    )(velocity)


def solution(mesh):
    n, m = mesh.shape["wall"], mesh.shape["span"]
    spec = P(None, "wall", "span", None)
    return jax.shard_map(
        functools.partial(body, n, m), mesh=mesh, in_specs=(spec,), out_specs=spec, check_vma=False
    )
```

```python
import functools

import jax
import jax.numpy as jnp
from jax import lax
from jax.experimental import pallas as pl
from jax.experimental.pallas import tpu as pltpu
from jax.sharding import PartitionSpec as P

visc_base = 4000.0
smag_gain = 2000.0
adv_step = 0.2

MESH = pl.DeviceIdType.MESH
TILE = 8


def inverse(x):
    guess = pl.reciprocal(x, approx=True)
    return guess * (2.0 - x * guess)


def kernel(
    n, m, vel, out, ext, zsend, zlo, zhi, fac_u, fac_p, fac_s, part, parts, ends, sides, planes,
    load_sem, zs_sem, zr_sem, ys_sem, yr_sem, ps_sem, pr_sem, es_sem, er_sem,
):
    _, ny, nz, nx = vel.shape
    rows = nz // n
    me = lax.axis_index("wall")
    mine = lax.axis_index("span")
    def peer(hop):
        if n & (n - 1):
            return lax.rem(me + hop, n)
        other = me
        for bit in (1 << i for i in range(n.bit_length() - 1)):
            if (n - hop) & bit:
                other = other + bit - 2 * bit * ((me // bit) % 2)
        return other

    after, before = lax.rem(mine + 1, m), lax.rem(mine + m - 1, m)

    load = pltpu.make_async_copy(vel, ext.at[:, pl.ds(1, ny), pl.ds(TILE, nz)], load_sem)
    load.start()

    barrier = pltpu.get_barrier_semaphore()
    for hop in range(1, n):
        pl.semaphore_signal(barrier, inc=1, device_id={"wall": peer(hop)}, device_id_type=MESH)
    for side in (after, before):
        pl.semaphore_signal(barrier, inc=1, device_id={"span": side}, device_id_type=MESH)

    load.wait()
    for c in range(3):
        zsend[0, c] = ext[c, pl.ds(1, ny), TILE, :]
        zsend[1, c] = ext[c, pl.ds(1, ny), TILE + nz - 1, :]
    pl.semaphore_wait(barrier, n + 1)
    to_after = pltpu.make_async_remote_copy(
        zsend.at[1], zlo, zs_sem.at[1], zr_sem.at[1],
        device_id={"span": after}, device_id_type=MESH,
    )
    to_before = pltpu.make_async_remote_copy(
        zsend.at[0], zhi, zs_sem.at[0], zr_sem.at[0],
        device_id={"span": before}, device_id_type=MESH,
    )
    to_after.start()
    to_before.start()

    up = pltpu.make_async_remote_copy(
        vel.at[:, ny - 1], ext.at[:, 0, pl.ds(TILE, nz)], ys_sem.at[0], yr_sem.at[0],
        device_id={"wall": jnp.minimum(me + 1, n - 1)}, device_id_type=MESH,
    )
    down = pltpu.make_async_remote_copy(
        vel.at[:, 0], ext.at[:, ny + 1, pl.ds(TILE, nz)], ys_sem.at[1], yr_sem.at[1],
        device_id={"wall": jnp.maximum(me - 1, 0)}, device_id_type=MESH,
    )
    has_above = me < n - 1
    has_below = me > 0
    pl.when(has_above)(up.start)
    pl.when(has_below)(down.start)

    def prepare(y, z):
        v, hx, hy, hz = [], [], [], []
        for c in range(3):
            here = ext[c, y + 1, z + TILE : z + 2 * TILE]
            v.append(here)
            hx.append(pltpu.roll(here, nx - 1, 1) - pltpu.roll(here, 1, 1))
            hy.append(
                ext[c, y + 2, z + TILE : z + 2 * TILE] - ext[c, y, z + TILE : z + 2 * TILE]
            )
            hz.append(
                ext[c, y + 1, z + TILE + 1 : z + 2 * TILE + 1]
                - ext[c, y + 1, z + TILE - 1 : z + 2 * TILE - 1]
            )
        xy = hx[1] + hy[0]
        xz = hx[2] + hz[0]
        yz = hy[2] + hz[1]
        squares = 2.0 * (hx[0] * hx[0] + hy[1] * hy[1] + hz[2] * hz[2])
        squares = squares + (xy * xy + xz * xz + yz * yz)
        strain = squares * lax.rsqrt(jnp.maximum(squares, 1e-30))
        e = inverse(visc_base + (0.5 * smag_gain) * strain)
        f = []
        for c in range(3):
            advect = v[0] * hx[c] + v[1] * hy[c] + v[2] * hz[c]
            f.append((v[c] - (0.5 * adv_step) * advect) * e)
        return e, f

    def step(y, z, carry):
        w, p, left, s, a = carry
        e, f = prepare(y, z)
        t = e + w
        u = inverse(1.0 + t)
        w = t * u
        s = tuple((s[c] + f[c]) * u for c in range(3))
        a = tuple(a[c] + p * s[c] for c in range(3))
        p_new = p * u
        left = left - p * p_new
        fac_u[y, z : z + TILE] = u
        fac_p[y, z : z + TILE] = p_new
        for c in range(3):
            fac_s[c, y, z : z + TILE] = s[c]
        return w, p_new, left, s, a

    one = jnp.ones((TILE, nx), jnp.float32)
    zero = jnp.zeros((TILE, nx), jnp.float32)
    start = (one, one, one, (zero,) * 3, (zero,) * 3)
    burst = 3 if (ny - 2) % 3 == 0 else 1

    def sweep(zs):
        def some(i, carries):
            for k in range(burst):
                carries = tuple(
                    step(1 + i * burst + k, z, carry) for z, carry in zip(zs, carries)
                )
            return carries

        return lax.fori_loop(0, (ny - 2) // burst, some, (start,) * len(zs))

    inner = tuple(range(TILE, nz - TILE, TILE))
    outer = (0, nz - TILE)
    carries = dict(zip(inner, sweep(inner)))

    to_after.wait_recv()
    to_before.wait_recv()
    for c in range(3):
        ext[c, pl.ds(1, ny), TILE - 1, :] = zlo[c]
        ext[c, pl.ds(1, ny), TILE + nz, :] = zhi[c]
    carries.update(zip(outer, sweep(outer)))

    @pl.when(has_above)
    def _():
        down.wait_recv()

    @pl.when(has_below)
    def _():
        up.wait_recv()

    @pl.when(jnp.logical_not(has_above))
    def _():
        ext[:, ny + 1, TILE : TILE + nz] = jnp.zeros((3, nz, nx), jnp.float32)

    @pl.when(jnp.logical_not(has_below))
    def _():
        ext[:, 0, TILE : TILE + nz] = jnp.zeros((3, nz, nx), jnp.float32)

    for z in range(0, nz, TILE):
        w, p, left, s, a = step(ny - 1, z, carries[z])
        e, f = prepare(0, z)
        values = (e + left, w, p, *s, *(f[c] + a[c] for c in range(3)))
        for k in range(z // rows, (z + TILE) // rows):
            for j, value in enumerate(values):
                part[k, j * rows : (j + 1) * rows] = value[k * rows - z : (k + 1) * rows - z]

    def spread(src, dst, send, recv):
        copies = []
        for hop in range(1, n):
            to = peer(hop)
            copies.append(
                pltpu.make_async_remote_copy(
                    src.at[to], dst.at[me], send.at[to], recv.at[me],
                    device_id={"wall": to}, device_id_type=MESH,
                )
            )
        return copies

    def arrived(src, dst, send, recv, k):
        @pl.when(me != k)
        def _():
            pltpu.make_async_remote_copy(
                src.at[k], dst.at[k], send.at[k], recv.at[k],
                device_id={"wall": k}, device_id_type=MESH,
            ).wait_recv()

    first = spread(part, parts, ps_sem, pr_sem)
    for copy in first:
        copy.start()
    parts[me] = part[me]

    def item(k, j):
        return parts[k, j * rows : (j + 1) * rows]

    ratios, shifts = [], []
    for k in range(n):
        arrived(part, parts, ps_sem, pr_sem, k)
        if k == 0:
            scale = inverse(item(0, 0) + 1.0)
            shift = [item(0, 6 + c) * scale for c in range(3)]
        else:
            p_low = item(k - 1, 2)
            scale = inverse(item(k, 0) + (item(k - 1, 1) - p_low * ratios[-1]))
            shift = [
                (item(k, 6 + c) + item(k - 1, 3 + c) + p_low * shifts[-1][c]) * scale
                for c in range(3)
            ]
        ratios.append(item(k, 2) * scale)
        shifts.append(shift)
    above = [jnp.zeros((rows, nx), jnp.float32)] * 3
    for k in reversed(range(n)):
        here = [shifts[k][c] + ratios[k] * above[c] for c in range(3)]
        for c in range(3):
            ends[k, c * rows : (c + 1) * rows] = here[c]
            ends[k, (3 + c) * rows : (4 + c) * rows] = above[c]
        above = here
    second = spread(ends, sides, es_sem, er_sem)
    for copy in second:
        copy.start()
    sides[me] = ends[me]
    for k in range(n):
        arrived(ends, sides, es_sem, er_sem, k)
        for j in range(6):
            planes[j, k * rows : (k + 1) * rows] = sides[k, j * rows : (j + 1) * rows]

    base = tuple(planes[c] for c in range(3))

    def back(i, x):
        y = ny - 1 - i
        u = fac_u[y]
        p = fac_p[y]
        x = tuple(fac_s[c, y] + p * base[c] + u * x[c] for c in range(3))
        for c in range(3):
            out[c, y] = x[c]
        return x

    lax.fori_loop(0, ny - 1, back, tuple(planes[3 + c] for c in range(3)))
    for c in range(3):
        out[c, 0] = base[c]

    to_after.wait_send()
    to_before.wait_send()
    pl.when(has_above)(up.wait_send)
    pl.when(has_below)(down.wait_send)
    for copy in first + second:
        copy.wait_send()


def body(n, m, velocity):
    _, ny, nz, nx = velocity.shape
    rows = nz // n
    f32 = jnp.float32
    dma = pltpu.SemaphoreType.DMA
    return pl.pallas_call(
        functools.partial(kernel, n, m),
        out_shape=jax.ShapeDtypeStruct(velocity.shape, f32),
        in_specs=[pl.BlockSpec(memory_space=pltpu.HBM)],
        out_specs=pl.BlockSpec(memory_space=pltpu.VMEM),
        scratch_shapes=[
            pltpu.VMEM((3, ny + 2, nz + 2 * TILE, nx), f32),
            pltpu.VMEM((2, 3, ny, nx), f32),
            pltpu.VMEM((3, ny, nx), f32),
            pltpu.VMEM((3, ny, nx), f32),
            pltpu.VMEM((ny, nz, nx), f32),
            pltpu.VMEM((ny, nz, nx), f32),
            pltpu.VMEM((3, ny, nz, nx), f32),
            pltpu.VMEM((n, 9 * rows, nx), f32),
            pltpu.VMEM((n, 9 * rows, nx), f32),
            pltpu.VMEM((n, 6 * rows, nx), f32),
            pltpu.VMEM((n, 6 * rows, nx), f32),
            pltpu.VMEM((6, nz, nx), f32),
            dma,
            dma((2,)),
            dma((2,)),
            dma((2,)),
            dma((2,)),
            dma((n,)),
            dma((n,)),
            dma((n,)),
            dma((n,)),
        ],
        compiler_params=pltpu.CompilerParams(
            collective_id=0, has_side_effects=True, vmem_limit_bytes=52 * 1024 * 1024
        ),
        name="channel",
    )(velocity)


def solution(mesh):
    n, m = mesh.shape["wall"], mesh.shape["span"]
    spec = P(None, "wall", "span", None)
    return jax.shard_map(
        functools.partial(body, n, m), mesh=mesh, in_specs=(spec,), out_specs=spec, check_vma=False
    )
```

```python
import functools

import jax
import jax.numpy as jnp
from jax import lax
from jax.experimental import pallas as pl
from jax.experimental.pallas import tpu as pltpu
from jax.sharding import PartitionSpec as P

visc_base = 4000.0
smag_gain = 2000.0
adv_step = 0.2

MESH = pl.DeviceIdType.MESH
TILE = 8


def inverse(x):
    guess = pl.reciprocal(x, approx=True)
    return guess * (2.0 - x * guess)


def kernel(
    n, m, vel, out, ext, zsend, zlo, zhi, fac_u, fac_p, fac_s, part, parts, ends, sides, planes,
    load_sem, zs_sem, zr_sem, ys_sem, yr_sem, ps_sem, pr_sem, es_sem, er_sem,
):
    _, ny, nz, nx = vel.shape
    rows = nz // n
    me = lax.axis_index("wall")
    mine = lax.axis_index("span")
    def peer(hop):
        if n & (n - 1):
            return lax.rem(me + hop, n)
        other, turn = me, n - hop
        turn = turn ^ 1 if turn > 1 else turn
        for bit in (1 << i for i in range(n.bit_length() - 1)):
            if turn & bit:
                other = other + bit - 2 * bit * ((me // bit) % 2)
        return other

    after, before = lax.rem(mine + 1, m), lax.rem(mine + m - 1, m)

    load = pltpu.make_async_copy(vel, ext.at[:, pl.ds(1, ny), pl.ds(TILE, nz)], load_sem)
    load.start()

    barrier = pltpu.get_barrier_semaphore()
    for hop in range(1, n):
        pl.semaphore_signal(barrier, inc=1, device_id={"wall": peer(hop)}, device_id_type=MESH)
    for side in (after, before):
        pl.semaphore_signal(barrier, inc=1, device_id={"span": side}, device_id_type=MESH)

    load.wait()
    for c in range(3):
        zsend[0, c] = ext[c, pl.ds(1, ny), TILE, :]
        zsend[1, c] = ext[c, pl.ds(1, ny), TILE + nz - 1, :]
    pl.semaphore_wait(barrier, n + 1)
    to_after = pltpu.make_async_remote_copy(
        zsend.at[1], zlo, zs_sem.at[1], zr_sem.at[1],
        device_id={"span": after}, device_id_type=MESH,
    )
    to_before = pltpu.make_async_remote_copy(
        zsend.at[0], zhi, zs_sem.at[0], zr_sem.at[0],
        device_id={"span": before}, device_id_type=MESH,
    )
    to_after.start()
    to_before.start()

    up = pltpu.make_async_remote_copy(
        ext.at[:, ny, pl.ds(TILE, nz)], ext.at[:, 0, pl.ds(TILE, nz)], ys_sem.at[0], yr_sem.at[0],
        device_id={"wall": jnp.minimum(me + 1, n - 1)}, device_id_type=MESH,
    )
    down = pltpu.make_async_remote_copy(
        ext.at[:, 1, pl.ds(TILE, nz)], ext.at[:, ny + 1, pl.ds(TILE, nz)], ys_sem.at[1], yr_sem.at[1],
        device_id={"wall": jnp.maximum(me - 1, 0)}, device_id_type=MESH,
    )
    has_above = me < n - 1
    has_below = me > 0
    pl.when(has_above)(up.start)
    pl.when(has_below)(down.start)

    def prepare(y, z):
        v, hx, hy, hz = [], [], [], []
        for c in range(3):
            here = ext[c, y + 1, z + TILE : z + 2 * TILE]
            v.append(here)
            hx.append(pltpu.roll(here, nx - 1, 1) - pltpu.roll(here, 1, 1))
            hy.append(
                ext[c, y + 2, z + TILE : z + 2 * TILE] - ext[c, y, z + TILE : z + 2 * TILE]
            )
            hz.append(
                ext[c, y + 1, z + TILE + 1 : z + 2 * TILE + 1]
                - ext[c, y + 1, z + TILE - 1 : z + 2 * TILE - 1]
            )
        xy = hx[1] + hy[0]
        xz = hx[2] + hz[0]
        yz = hy[2] + hz[1]
        squares = 2.0 * (hx[0] * hx[0] + hy[1] * hy[1] + hz[2] * hz[2])
        squares = squares + (xy * xy + xz * xz + yz * yz)
        strain = squares * lax.rsqrt(jnp.maximum(squares, 1e-30))
        e = inverse(visc_base + (0.5 * smag_gain) * strain)
        f = []
        for c in range(3):
            advect = v[0] * hx[c] + v[1] * hy[c] + v[2] * hz[c]
            f.append((v[c] - (0.5 * adv_step) * advect) * e)
        return e, f

    def step(y, z, carry):
        w, p, left, s, a = carry
        e, f = prepare(y, z)
        t = e + w
        u = inverse(1.0 + t)
        w = t * u
        s = tuple((s[c] + f[c]) * u for c in range(3))
        a = tuple(a[c] + p * s[c] for c in range(3))
        p_new = p * u
        left = left - p * p_new
        fac_u[y, z : z + TILE] = u
        fac_p[y, z : z + TILE] = p_new
        for c in range(3):
            fac_s[c, y, z : z + TILE] = s[c]
        return w, p_new, left, s, a

    one = jnp.ones((TILE, nx), jnp.float32)
    zero = jnp.zeros((TILE, nx), jnp.float32)
    start = (one, one, one, (zero,) * 3, (zero,) * 3)
    burst = 3 if (ny - 2) % 3 == 0 else 1

    def sweep(zs):
        def some(i, carries):
            for k in range(burst):
                carries = tuple(
                    step(1 + i * burst + k, z, carry) for z, carry in zip(zs, carries)
                )
            return carries

        return lax.fori_loop(0, (ny - 2) // burst, some, (start,) * len(zs))

    inner = tuple(range(TILE, nz - TILE, TILE))
    outer = (0, nz - TILE)
    carries = dict(zip(inner, sweep(inner)))

    to_after.wait_recv()
    to_before.wait_recv()
    for c in range(3):
        ext[c, pl.ds(1, ny), TILE - 1, :] = zlo[c]
        ext[c, pl.ds(1, ny), TILE + nz, :] = zhi[c]
    carries.update(zip(outer, sweep(outer)))

    @pl.when(has_above)
    def _():
        down.wait_recv()

    @pl.when(has_below)
    def _():
        up.wait_recv()

    @pl.when(jnp.logical_not(has_above))
    def _():
        ext[:, ny + 1, TILE : TILE + nz] = jnp.zeros((3, nz, nx), jnp.float32)

    @pl.when(jnp.logical_not(has_below))
    def _():
        ext[:, 0, TILE : TILE + nz] = jnp.zeros((3, nz, nx), jnp.float32)

    for z in range(0, nz, TILE):
        w, p, left, s, a = step(ny - 1, z, carries[z])
        e, f = prepare(0, z)
        values = (e + left, w, p, *s, *(f[c] + a[c] for c in range(3)))
        for k in range(z // rows, (z + TILE) // rows):
            for j, value in enumerate(values):
                part[k, j * rows : (j + 1) * rows] = value[k * rows - z : (k + 1) * rows - z]

    def spread(src, dst, send, recv):
        copies = []
        for hop in range(1, n):
            to = peer(hop)
            copies.append(
                pltpu.make_async_remote_copy(
                    src.at[to], dst.at[me], send.at[to], recv.at[me],
                    device_id={"wall": to}, device_id_type=MESH,
                )
            )
        return copies

    def arrived(src, dst, send, recv, k):
        @pl.when(me != k)
        def _():
            pltpu.make_async_remote_copy(
                src.at[k], dst.at[k], send.at[k], recv.at[k],
                device_id={"wall": k}, device_id_type=MESH,
            ).wait_recv()

    first = spread(part, parts, ps_sem, pr_sem)
    for copy in first:
        copy.start()
    parts[me] = part[me]

    def item(k, j):
        return parts[k, j * rows : (j + 1) * rows]

    ratios, shifts = [], []
    for k in range(n):
        arrived(part, parts, ps_sem, pr_sem, k)
        if k == 0:
            scale = inverse(item(0, 0) + 1.0)
            shift = [item(0, 6 + c) * scale for c in range(3)]
        else:
            p_low = item(k - 1, 2)
            scale = inverse(item(k, 0) + (item(k - 1, 1) - p_low * ratios[-1]))
            shift = [
                (item(k, 6 + c) + item(k - 1, 3 + c) + p_low * shifts[-1][c]) * scale
                for c in range(3)
            ]
        ratios.append(item(k, 2) * scale)
        shifts.append(shift)
    above = [jnp.zeros((rows, nx), jnp.float32)] * 3
    for k in reversed(range(n)):
        here = [shifts[k][c] + ratios[k] * above[c] for c in range(3)]
        for c in range(3):
            ends[k, c * rows : (c + 1) * rows] = here[c]
            ends[k, (3 + c) * rows : (4 + c) * rows] = above[c]
        above = here
    second = spread(ends, sides, es_sem, er_sem)
    for copy in second:
        copy.start()
    sides[me] = ends[me]
    for k in range(n):
        arrived(ends, sides, es_sem, er_sem, k)
        for j in range(6):
            planes[j, k * rows : (k + 1) * rows] = sides[k, j * rows : (j + 1) * rows]

    base = tuple(planes[c] for c in range(3))

    def back(i, x):
        y = ny - 1 - i
        u = fac_u[y]
        p = fac_p[y]
        x = tuple(fac_s[c, y] + p * base[c] + u * x[c] for c in range(3))
        for c in range(3):
            out[c, y] = x[c]
        return x

    lax.fori_loop(0, ny - 1, back, tuple(planes[3 + c] for c in range(3)))
    for c in range(3):
        out[c, 0] = base[c]

    to_after.wait_send()
    to_before.wait_send()
    pl.when(has_above)(up.wait_send)
    pl.when(has_below)(down.wait_send)
    for copy in first + second:
        copy.wait_send()


def body(n, m, velocity):
    _, ny, nz, nx = velocity.shape
    rows = nz // n
    f32 = jnp.float32
    dma = pltpu.SemaphoreType.DMA
    return pl.pallas_call(
        functools.partial(kernel, n, m),
        out_shape=jax.ShapeDtypeStruct(velocity.shape, f32),
        in_specs=[pl.BlockSpec(memory_space=pltpu.HBM)],
        out_specs=pl.BlockSpec(memory_space=pltpu.VMEM),
        scratch_shapes=[
            pltpu.VMEM((3, ny + 2, nz + 2 * TILE, nx), f32),
            pltpu.VMEM((2, 3, ny, nx), f32),
            pltpu.VMEM((3, ny, nx), f32),
            pltpu.VMEM((3, ny, nx), f32),
            pltpu.VMEM((ny, nz, nx), f32),
            pltpu.VMEM((ny, nz, nx), f32),
            pltpu.VMEM((3, ny, nz, nx), f32),
            pltpu.VMEM((n, 9 * rows, nx), f32),
            pltpu.VMEM((n, 9 * rows, nx), f32),
            pltpu.VMEM((n, 6 * rows, nx), f32),
            pltpu.VMEM((n, 6 * rows, nx), f32),
            pltpu.VMEM((6, nz, nx), f32),
            dma,
            dma((2,)),
            dma((2,)),
            dma((2,)),
            dma((2,)),
            dma((n,)),
            dma((n,)),
            dma((n,)),
            dma((n,)),
        ],
        compiler_params=pltpu.CompilerParams(
            collective_id=0, has_side_effects=True, vmem_limit_bytes=52 * 1024 * 1024
        ),
        name="channel",
    )(velocity)


def solution(mesh):
    n, m = mesh.shape["wall"], mesh.shape["span"]
    spec = P(None, "wall", "span", None)
    return jax.shard_map(
        functools.partial(body, n, m), mesh=mesh, in_specs=(spec,), out_specs=spec, check_vma=False
    )
```
